32 devices in a mesh: groups: 2 (over y), param: 4 (over z), dp: 4 (over x, core).
Axes of the slice: x: 2, y: 2, z: 4, core: 2. Of those that a mesh axis runs over, the one named last changes fastest.
Arguments:
- acts: bfloat16 [8, 4096, 8192], P('groups', 'dp', 'param'), parts along dimension 0, may hold values from -6 to 6
- grads: bfloat16 [8, 4096, 16384], P('groups', 'dp', 'param'), parts along dimension 0, may hold values from -6 to 6
- lengths: int32 [8], P('groups'), parts along dimension 0, may hold values from 1024 to 4096, as said below
- row_sign: int32 [8192], P('param'), may hold values from 0 to 1
- col_sign: int32 [16384], P('param'), may hold values from 0 to 1
- row_index: int32 [64], replicated, may hold values from 0 to 8191
- col_index: int32 [128], replicated, may hold values from 0 to 16383
Outputs:
- sketch: float32 [8, 64, 128], P('groups', 'param', 'dp'), parts along dimension 0
The draws below stay inside these ranges and needn't reach their ends.
There are 2 independent parts, one for each index of `groups`. The reference program is written for one: setup_inputs(seed, part) draws one part's arguments, and reference() takes and returns one part's arrays. A program takes and returns all parts, laid end to end along the dimension named above; an argument that names none is the same for every part. Nothing has to cross between parts.
Inputs may be any that keep to these rules, and one draw needn't show every extreme that they name: `lengths`: some example has all 4096 tokens live.
All inputs are finite; a program needn't handle non-finite values.
Results may differ from the reference program's by a relative error of at most 0.0003.
Values sent between devices are 32-bit elements; how exact they have to be, the bound alone decides.
A program may use at most 128 MiB of HBM per device.

```python
import jax
import jax.numpy as jnp
from jax import lax

D = 8192
F = 16384
EX = 4
KA = 64
KB = 128
SEQ = 4096


def draw_lengths(key, part):
    key = jax.random.fold_in(key, 7)
    first, second = jax.random.split(key)
    values = jax.random.randint(first, (EX,), SEQ // 4, SEQ + 1)
    chosen = jax.random.randint(second, (), 0, EX)
    return jnp.where(jnp.arange(EX) == chosen, SEQ, values).astype(jnp.int32)


def place_ends(values, own_key, smallest, high):
    spot = [jax.random.randint(jax.random.fold_in(own_key, axis), (), 0, length) for axis, length in enumerate(values.shape)]
    main_axis = values.shape.index(max(values.shape))
    neighbour = spot[:main_axis] + [(spot[main_axis] + 1) % values.shape[main_axis]] + spot[main_axis + 1:]
    return values.at[tuple(spot)].set(smallest).at[tuple(neighbour)].set(high)


def levels(key, shape, cuts, low, top_value):
    def one(dim, parts):
        draws = jax.random.uniform(jax.random.fold_in(jax.random.fold_in(key, 6), dim), (parts,), jnp.float32, low / len(cuts), top_value / len(cuts))
        return jnp.repeat(jnp.exp(draws), shape[dim] // parts).reshape((-1,) + (1,) * (len(shape) - dim - 1))

    level = one(*cuts[0])
    for cut in cuts[1:]:
        level = level * one(*cut)
    return level


def gaussian(stream_key, extent, scale, most, shards=(), held_as=jnp.bfloat16):
    gain = levels(stream_key, extent, shards, -0.22, 0.18) if shards else 1.0
    values = jax.random.normal(stream_key, extent, jnp.float32) * scale * gain
    return jnp.minimum(jnp.maximum(values, -most), most).astype(held_as)


def setup_inputs(seed: int = 0, part: int = 0) -> dict:
    key_of = jax.random.split(jax.random.key(seed), 8)
    part_splits = jax.random.split(jax.random.fold_in(key_of[7], part), 8)
    acts = gaussian(part_splits[0], (EX, SEQ, D), 1.0, 6.0, ((1, 4), (2, 4)))
    grads = gaussian(part_splits[1], (EX, SEQ, F), 1.0, 6.0, ((1, 4), (2, 4)))
    lengths = draw_lengths(jax.random.fold_in(jax.random.fold_in(key_of[7], part), 71), part)
    row_sign = place_ends(jax.random.randint(key_of[3], (D,), 0, 2), jax.random.fold_in(key_of[3], 1), 0, 1).astype(jnp.int32)
    col_sign = place_ends(jax.random.randint(key_of[4], (F,), 0, 2), jax.random.fold_in(key_of[4], 1), 0, 1).astype(jnp.int32)
    row_index = place_ends(jax.random.randint(key_of[5], (KA,), 0, D), jax.random.fold_in(key_of[5], 1), 0, D - 1).astype(jnp.int32)
    col_index = place_ends(jax.random.randint(key_of[6], (KB,), 0, F), jax.random.fold_in(key_of[6], 1), 0, F - 1).astype(jnp.int32)
    return dict(acts=acts, grads=grads, lengths=lengths, row_sign=row_sign, col_sign=col_sign, row_index=row_index, col_index=col_index)


def bit_parity(values):
    folded = values
    for shift in (16, 8, 4, 2, 1):
        folded = jnp.bitwise_xor(folded, jnp.right_shift(folded, shift))
    return jnp.bitwise_and(folded, 1)


def hadamard_table(indices, width):
    columns = jnp.arange(width, dtype=jnp.int32)
    parity = bit_parity(jnp.bitwise_and(columns[:, None], indices[None, :].astype(jnp.int32)))
    return (1 - 2 * parity).astype(jnp.float32)


def reference(acts, grads, lengths, row_sign, col_sign, row_index, col_index):
    row_table = hadamard_table(row_index, D)
    col_table = hadamard_table(col_index, F)
    row_flip = (1 - 2 * row_sign).astype(jnp.float32)
    col_flip = (1 - 2 * col_sign).astype(jnp.float32)
    position = jnp.arange(SEQ, dtype=jnp.int32)

    def one_example(items):
        example_acts, example_grads, length = items
        live = (position < length).astype(jnp.float32)
        masked = (example_acts.astype(jnp.float32) * row_flip[None, :] * live[:, None]).astype(jnp.bfloat16)
        flipped = (example_grads.astype(jnp.float32) * col_flip[None, :]).astype(jnp.bfloat16)
        rows_mixed = jnp.dot(masked.astype(jnp.float32), row_table, precision=lax.Precision.HIGHEST) * (1.0 / D ** 0.5)
        cols_mixed = jnp.dot(flipped.astype(jnp.float32), col_table, precision=lax.Precision.HIGHEST) * (1.0 / F ** 0.5)
        return jnp.dot(rows_mixed.T, cols_mixed, precision=lax.Precision.HIGHEST) * (1.0 / SEQ ** 0.5)

    return lax.map(one_example, (acts, grads, lengths))
```

```python
import jax
import jax.numpy as jnp
from jax import lax
from jax.sharding import PartitionSpec as P

D = 8192
F = 16384


def bit_parity(values):
    folded = values
    for shift in (16, 8, 4, 2, 1):
        folded = jnp.bitwise_xor(folded, jnp.right_shift(folded, shift))
    return jnp.bitwise_and(folded, 1)


def hadamard_block(indices, offset, width):
    columns = offset + jnp.arange(width, dtype=jnp.int32)
    parity = bit_parity(jnp.bitwise_and(columns[:, None], indices[None, :]))
    return (1 - 2 * parity).astype(jnp.bfloat16)


def local(acts, grads, lengths, row_sign, col_sign, row_index, col_index):
    tok_block = acts.shape[1]
    row_block = acts.shape[2]
    col_block = grads.shape[2]
    param_pos = lax.axis_index("param")
    data_pos = lax.axis_index("dp")
    data_count = lax.axis_size("dp")
    position = data_pos * tok_block + jnp.arange(tok_block, dtype=jnp.int32)
    live = position[None, :] < lengths[:, None]
    row_flip = (1 - 2 * row_sign).astype(jnp.bfloat16)
    col_flip = (1 - 2 * col_sign).astype(jnp.bfloat16)
    masked = jnp.where(
        live[:, :, None], acts * row_flip[None, None, :], jnp.zeros((), jnp.bfloat16)
    )
    flipped = grads * col_flip[None, None, :]
    row_table = hadamard_block(row_index, param_pos * row_block, row_block)
    col_table = hadamard_block(col_index, param_pos * col_block, col_block)
    rows_term = jnp.einsum("etd,dk->etk", masked, row_table, preferred_element_type=jnp.float32) * (
        1.0 / D**0.5
    )
    cols_term = jnp.einsum(
        "etd,dk->etk", flipped, col_table, preferred_element_type=jnp.float32
    ) * (1.0 / F**0.5)
    final_scale = 1.0 / (tok_block * data_count) ** 0.5
    rows_mixed = lax.psum(rows_term, "param")
    partial_sketch = jnp.einsum(
        "etk,etl->ekl", rows_mixed, cols_term, precision=lax.Precision.HIGHEST
    )
    partial_sketch = lax.psum_scatter(partial_sketch, "param", scatter_dimension=1, tiled=True)
    summed = lax.psum_scatter(partial_sketch, "dp", scatter_dimension=2, tiled=True)
    return summed * final_scale


def solution(mesh):
    placed = (
        P("groups", "dp", "param"),
        P("groups", "dp", "param"),
        P("groups"),
        P("param"),
        P("param"),
        P(),
        P(),
    )
    return jax.shard_map(
        local, mesh=mesh, in_specs=placed, out_specs=P("groups", "param", "dp"), check_vma=False
    )
```

```python
import functools

import jax
import jax.numpy as jnp
from jax import lax
from jax.experimental import pallas as pl
from jax.experimental.pallas import tpu as pltpu
from jax.sharding import PartitionSpec as P

D = 8192
F = 16384
BLK = 512
HALF = BLK // 2
SUB = HALF // 2
LAG = 2
SLOTS = 4


def signed_table(indices, sign, offset, width):
    columns = offset + jnp.arange(width, dtype=jnp.int32)
    bits = lax.population_count(jnp.bitwise_and(columns[:, None], indices[None, :]))
    parity = jnp.bitwise_and(bits + sign[:, None], 1)
    return (1 - 2 * parity).astype(jnp.bfloat16)


def split(x):
    hi = x.astype(jnp.bfloat16)
    return hi, (x - hi.astype(jnp.float32)).astype(jnp.bfloat16)


def dot(a, b):
    return jnp.dot(a, b, preferred_element_type=jnp.float32)


def kernel(zn, dn, scale, lengths, rtab, ctab, acts, grads, out, abuf, gbuf, own, pin, sin,
           pout, sout, chi, clo, acc, part, part_in, ybuf, zbuf, zin, asem, gsem, psend, precv,
           ssend, srecv, dsend, drecv, zsend, zrecv):
    z = lax.axis_index("param")
    d = lax.axis_index("dp")
    examples, tokens, _ = acts.shape
    per = tokens // BLK
    blocks = examples * per
    chunks = 2 * blocks
    tail = LAG * (zn - 1) // 2
    cm = part.shape[2]
    rm = zbuf.shape[1]
    ka = 64

    def fetch(src, buf, sem, j):
        slot = lax.rem(j, SLOTS)
        rows = pl.ds(pl.multiple_of(lax.rem(j, per) * BLK, BLK), BLK)
        return pltpu.make_async_copy(src.at[j // per, rows, :], buf.at[slot], sem.at[slot])

    for j in range(min(SLOTS, blocks)):
        fetch(acts, abuf, asem, jnp.int32(j)).start()
        fetch(grads, gbuf, gsem, jnp.int32(j)).start()

    barrier = pltpu.get_barrier_semaphore()
    for off in range(1, zn):
        pl.semaphore_signal(barrier, inc=1, device_id={"param": lax.rem(z + off, zn)},
                            device_id_type=pl.DeviceIdType.MESH)
    for off in range(1, dn):
        pl.semaphore_signal(barrier, inc=1, device_id={"dp": lax.rem(d + off, dn)},
                            device_id_type=pl.DeviceIdType.MESH)
    pl.semaphore_wait(barrier, zn - 1 + dn - 1)

    def up(k):
        return pltpu.make_async_remote_copy(
            src_ref=pout.at[k], dst_ref=pin.at[k], send_sem=psend.at[k], recv_sem=precv.at[k],
            device_id={"param": lax.rem(z + 1, zn)}, device_id_type=pl.DeviceIdType.MESH)

    def down(k):
        return pltpu.make_async_remote_copy(
            src_ref=sout.at[k], dst_ref=sin.at[k], send_sem=ssend.at[k], recv_sem=srecv.at[k],
            device_id={"param": lax.rem(z + zn - 1, zn)}, device_id_type=pl.DeviceIdType.MESH)

    def across(e, off):
        peer = lax.rem(d + off, dn)
        return pltpu.make_async_remote_copy(
            src_ref=part.at[e, peer], dst_ref=part_in.at[e, off - 1],
            send_sem=dsend.at[e, off - 1], recv_sem=drecv.at[e, off - 1],
            device_id={"dp": peer}, device_id_type=pl.DeviceIdType.MESH)

    def along(off):
        peer = lax.rem(z + off, zn)
        return pltpu.make_async_remote_copy(
            src_ref=zbuf.at[peer], dst_ref=zin.at[off - 1],
            send_sem=zsend.at[off - 1], recv_sem=zrecv.at[off - 1],
            device_id={"param": peer}, device_id_type=pl.DeviceIdType.MESH)

    def one_way(t, place, copy, arrived, leaving):
        k = t - LAG * place

        @pl.when(jnp.logical_and(k >= 0, k < chunks))
        def _():
            @pl.when(place > 0)
            def _():
                copy(k).wait_recv()

            @pl.when(place == 0)
            def _():
                arrived[k] = jnp.zeros((SUB, 128), jnp.float32)

            @pl.when(place < zn - 1)
            def _():
                leaving[k] = own[k] + arrived[k]
                copy(k).start()

    def exchange(t):
        one_way(t, z, up, pin, pout)
        one_way(t, zn - 1 - z, down, sin, sout)

    lane = lax.broadcasted_iota(jnp.int32, (HALF, 128), 1)
    row = lax.broadcasted_iota(jnp.int32, (HALF, 128), 0)
    place = d * tokens + row + jnp.where(lane >= ka, HALF, 0)

    def step(j, carry):
        @pl.when(j < blocks)
        def _():
            slot = lax.rem(j, SLOTS)
            fetch(acts, abuf, asem, j).wait()
            value = dot(abuf[slot, :HALF, :], rtab[:, :128])
            value = value + dot(abuf[slot, HALF:, :], rtab[:, 128:])
            live = place + lax.rem(j, per) * BLK < lengths[j // per]
            value = jnp.where(live, value, 0.0)
            own[2 * j] = value[:SUB]
            own[2 * j + 1] = value[SUB:]

            @pl.when(j + SLOTS < blocks)
            def _():
                fetch(acts, abuf, asem, j + SLOTS).start()

        exchange(2 * j)

        @pl.when(j < blocks)
        def _():
            slot = lax.rem(j, SLOTS)
            fetch(grads, gbuf, gsem, j).wait()
            for half in range(2):
                value = dot(gbuf[slot, half * HALF:(half + 1) * HALF, :], ctab[...])
                hi, lo = split(value.T)
                chi[j, half * 128:(half + 1) * 128, :] = hi
                clo[j, half * 128:(half + 1) * 128, :] = lo

            @pl.when(j + SLOTS < blocks)
            def _():
                fetch(grads, gbuf, gsem, j + SLOTS).start()

        exchange(2 * j + 1)

        @pl.when(j >= tail)
        def _():
            b = j - tail
            e = b // per
            h = lax.rem(b, per)
            total = jnp.concatenate(
                [own[2 * b + s] + pin[2 * b + s] + sin[2 * b + s] for s in range(2)], axis=0)
            hi, lo = split(total)
            value = dot(chi[b], hi) + (dot(chi[b], lo) + dot(clo[b], hi))

            @pl.when(h == 0)
            def _():
                acc[...] = value

            @pl.when(h > 0)
            def _():
                acc[...] += value

            @pl.when(h == per - 1)
            def _():
                lanes = lax.broadcasted_iota(jnp.int32, (128, 128), 1)
                both = jnp.where(lanes < ka, acc[:128, :], acc[128:, :])
                for p in range(dn):
                    part[e, p] = both[p * cm:(p + 1) * cm]
                for off in range(1, dn):
                    across(e, off).start()

        return carry

    lax.fori_loop(0, blocks + tail, step, 0)

    for e in range(examples):
        value = part[e, d]
        for off in range(1, dn):
            across(e, off).wait_recv()
            value = value + part_in[e, off - 1]
        ybuf[e * cm:(e + 1) * cm, :] = value
    turned = ybuf[...].T
    turned = turned[:ka] + turned[ka:]
    for p in range(zn):
        zbuf[p] = turned[p * rm:(p + 1) * rm]
    for off in range(1, zn):
        along(off).start()
    value = zbuf[z]
    for off in range(1, zn):
        along(off).wait_recv()
        value = value + zin[off - 1]
    value = value * scale
    for e in range(examples):
        out[e] = value[:, e * cm:(e + 1) * cm]

    for off in range(1, zn):
        along(off).wait_send()
    for e in range(examples):
        for off in range(1, dn):
            across(e, off).wait_send()

    def drain(k, carry):
        @pl.when(z < zn - 1)
        def _():
            up(k).wait_send()

        @pl.when(z > 0)
        def _():
            down(k).wait_send()

        return carry

    lax.fori_loop(0, chunks, drain, 0)


def local(acts, grads, lengths, row_sign, col_sign, row_index, col_index):
    examples, tokens, row_block = acts.shape
    col_block = grads.shape[2]
    z = lax.axis_index("param")
    zn = lax.axis_size("param")
    dn = lax.axis_size("dp")
    ka = row_index.shape[0]
    kb = col_index.shape[0]
    rm, cm = ka // zn, kb // dn
    rows = signed_table(row_index, row_sign, z * row_block, row_block)
    none = jnp.zeros_like(rows)
    rtab = jnp.concatenate([rows, none, none, rows], axis=1)
    ctab = signed_table(col_index, col_sign, z * col_block, col_block)
    scale = 1.0 / (D**0.5 * F**0.5 * (tokens * dn) ** 0.5)
    blocks = examples * tokens // BLK
    line = pltpu.VMEM((2 * blocks, SUB, 128), jnp.float32)
    dma = pltpu.SemaphoreType.DMA
    vmem = pl.BlockSpec(memory_space=pltpu.VMEM)
    hbm = pl.BlockSpec(memory_space=pl.ANY)
    return pl.pallas_call(
        functools.partial(kernel, zn, dn, scale),
        out_shape=jax.ShapeDtypeStruct((examples, rm, cm), jnp.float32),
        in_specs=[pl.BlockSpec(memory_space=pltpu.SMEM), vmem, vmem, hbm, hbm],
        out_specs=vmem,
        scratch_shapes=[
            pltpu.VMEM((SLOTS, BLK, row_block), jnp.bfloat16),
            pltpu.VMEM((SLOTS, BLK, col_block), jnp.bfloat16),
            line, line, line, line, line,
            pltpu.VMEM((blocks, 256, HALF), jnp.bfloat16),
            pltpu.VMEM((blocks, 256, HALF), jnp.bfloat16),
            pltpu.VMEM((256, 128), jnp.float32),
            pltpu.VMEM((examples, dn, cm, 128), jnp.float32),
            pltpu.VMEM((examples, dn - 1, cm, 128), jnp.float32),
            pltpu.VMEM((examples * cm, 128), jnp.float32),
            pltpu.VMEM((zn, rm, examples * cm), jnp.float32),
            pltpu.VMEM((zn - 1, rm, examples * cm), jnp.float32),
            dma((SLOTS,)), dma((SLOTS,)),
            dma((2 * blocks,)), dma((2 * blocks,)), dma((2 * blocks,)), dma((2 * blocks,)),
            dma((examples, dn - 1)), dma((examples, dn - 1)),
            dma((zn - 1,)), dma((zn - 1,)),
        ],
        compiler_params=pltpu.CompilerParams(
            collective_id=0, has_side_effects=True, vmem_limit_bytes=52 * 1024 * 1024
        ),
        cost_estimate=pl.CostEstimate(
            flops=2 * examples * tokens * (row_block * ka + col_block * kb),
            bytes_accessed=2 * examples * tokens * (row_block + col_block),
            transcendentals=0,
        ),
    )(lengths, rtab, ctab, acts, grads)


def solution(mesh):
    placed = (
        P("groups", "dp", "param"),
        P("groups", "dp", "param"),
        P("groups"),
        P("param"),
        P("param"),
        P(),
        P(),
    )
    return jax.shard_map(
        local, mesh=mesh, in_specs=placed, out_specs=P("groups", "param", "dp"), check_vma=False
    )
```

```python
import functools

import jax
import jax.numpy as jnp
from jax import lax
from jax.experimental import pallas as pl
from jax.experimental.pallas import tpu as pltpu
from jax.sharding import PartitionSpec as P

D = 8192
F = 16384
BLK = 512
HALF = BLK // 2
SUB = HALF // 2
LAG = 3
SLOTS = 4


def hadamard_signs(base, stride, count, index):
    values = base + stride * lax.broadcasted_iota(jnp.int32, (count, 128), 0)
    values = jnp.bitwise_and(values, index)
    for shift in (16, 8, 4, 2, 1):
        values = jnp.bitwise_xor(values, jnp.right_shift(values, shift))
    return (1 - 2 * jnp.bitwise_and(values, 1)).astype(jnp.float32)


def split(x):
    hi = x.astype(jnp.bfloat16)
    return hi, (x - hi.astype(jnp.float32)).astype(jnp.bfloat16)


def dot(a, b):
    return jnp.dot(a, b, preferred_element_type=jnp.float32)


def kernel(zn, dn, scale, lengths, rsign, csign, rindex, cindex, acts, grads, out, rtab, ctab, abuf, gbuf, own, pin, sin,
           pout, sout, chi, clo, acc, part, part_in, ybuf, zbuf, zin, asem, gsem, psend, precv,
           ssend, srecv, dsend, drecv, zsend, zrecv):
    z = lax.axis_index("param")
    d = lax.axis_index("dp")
    examples, tokens, _ = acts.shape
    per = tokens // BLK
    blocks = examples * per
    chunks = 2 * blocks
    tail = (LAG * (zn - 1) + 1) // 2
    cm = part.shape[2]
    rm = zbuf.shape[1]
    ka = 64

    def fetch(src, buf, sem, j):
        slot = lax.rem(j, SLOTS)
        rows = pl.ds(pl.multiple_of(lax.rem(j, per) * BLK, BLK), BLK)
        return pltpu.make_async_copy(src.at[j // per, rows, :], buf.at[slot], sem.at[slot])

    for j in range(min(SLOTS, blocks)):
        fetch(acts, abuf, asem, jnp.int32(j)).start()
        fetch(grads, gbuf, gsem, jnp.int32(j)).start()

    barrier = pltpu.get_barrier_semaphore()
    for off in range(1, zn):
        pl.semaphore_signal(barrier, inc=1, device_id={"param": lax.rem(z + off, zn)},
                            device_id_type=pl.DeviceIdType.MESH)
    for off in range(1, dn):
        pl.semaphore_signal(barrier, inc=1, device_id={"dp": lax.rem(d + off, dn)},
                            device_id_type=pl.DeviceIdType.MESH)
    def fill(sign, index, store):
        groups = sign.shape[0]
        high = hadamard_signs(z * groups * 128, 128, groups, index[...])
        low = hadamard_signs(0, 1, 128, index[...])
        flips = (1 - 2 * sign[...]).astype(jnp.float32).T
        for g in range(groups):
            store(g * 128, (low * high[g:g + 1, :]) * flips[:, g:g + 1])

    def store_rows(at, value):
        rtab[at:at + 128, :] = value.astype(jnp.bfloat16)

    def store_cols(at, value):
        ctab[at:at + 128, :] = value.astype(jnp.bfloat16)

    fill(rsign, rindex, store_rows)
    fill(csign, cindex, store_cols)
    pl.semaphore_wait(barrier, zn - 1 + dn - 1)

    def up(k):
        return pltpu.make_async_remote_copy(
            src_ref=pout.at[k], dst_ref=pin.at[k], send_sem=psend.at[k], recv_sem=precv.at[k],
            device_id={"param": lax.rem(z + 1, zn)}, device_id_type=pl.DeviceIdType.MESH)

    def down(k):
        return pltpu.make_async_remote_copy(
            src_ref=sout.at[k], dst_ref=sin.at[k], send_sem=ssend.at[k], recv_sem=srecv.at[k],
            device_id={"param": lax.rem(z + zn - 1, zn)}, device_id_type=pl.DeviceIdType.MESH)

    def across(e, off):
        peer = lax.rem(d + off, dn)
        return pltpu.make_async_remote_copy(
            src_ref=part.at[e, peer], dst_ref=part_in.at[e, off - 1],
            send_sem=dsend.at[e, off - 1], recv_sem=drecv.at[e, off - 1],
            device_id={"dp": peer}, device_id_type=pl.DeviceIdType.MESH)

    def along(off):
        peer = lax.rem(z + off, zn)
        return pltpu.make_async_remote_copy(
            src_ref=zbuf.at[peer], dst_ref=zin.at[off - 1],
            send_sem=zsend.at[off - 1], recv_sem=zrecv.at[off - 1],
            device_id={"param": peer}, device_id_type=pl.DeviceIdType.MESH)

    def one_way(t, place, copy, arrived, leaving):
        k = t - LAG * place

        @pl.when(jnp.logical_and(k >= 0, k < chunks))
        def _():
            @pl.when(place > 0)
            def _():
                copy(k).wait_recv()

            @pl.when(place == 0)
            def _():
                arrived[k] = jnp.zeros((SUB, 128), jnp.float32)

            @pl.when(place < zn - 1)
            def _():
                leaving[k] = own[k] + arrived[k]
                copy(k).start()

    def exchange(t):
        one_way(t, z, up, pin, pout)
        one_way(t, zn - 1 - z, down, sin, sout)

    lane = lax.broadcasted_iota(jnp.int32, (HALF, 128), 1)
    row = lax.broadcasted_iota(jnp.int32, (HALF, 128), 0)
    place = d * tokens + row + jnp.where(lane >= ka, HALF, 0)

    def step(j, carry):
        @pl.when(j < blocks)
        def _():
            slot = lax.rem(j, SLOTS)
            fetch(acts, abuf, asem, j).wait()
            value = jnp.where(
                lane < ka, dot(abuf[slot, :HALF, :], rtab[...]), dot(abuf[slot, HALF:, :], rtab[...])
            )
            live = place + lax.rem(j, per) * BLK < lengths[j // per]
            value = jnp.where(live, value, 0.0)
            own[2 * j] = value[:SUB]
            own[2 * j + 1] = value[SUB:]

            @pl.when(j + SLOTS < blocks)
            def _():
                fetch(acts, abuf, asem, j + SLOTS).start()

        exchange(2 * j)

        @pl.when(j < blocks)
        def _():
            slot = lax.rem(j, SLOTS)
            fetch(grads, gbuf, gsem, j).wait()
            for half in range(2):
                value = dot(gbuf[slot, half * HALF:(half + 1) * HALF, :], ctab[...])
                hi, lo = split(value.T)
                chi[j, half * 128:(half + 1) * 128, :] = hi
                clo[j, half * 128:(half + 1) * 128, :] = lo

            @pl.when(j + SLOTS < blocks)
            def _():
                fetch(grads, gbuf, gsem, j + SLOTS).start()

        exchange(2 * j + 1)

        @pl.when(j >= tail)
        def _():
            b = j - tail
            e = b // per
            h = lax.rem(b, per)
            total = jnp.concatenate(
                [own[2 * b + s] + pin[2 * b + s] + sin[2 * b + s] for s in range(2)], axis=0)
            hi, lo = split(total)
            value = dot(chi[b], hi) + (dot(chi[b], lo) + dot(clo[b], hi))

            @pl.when(h == 0)
            def _():
                acc[...] = value

            @pl.when(h > 0)
            def _():
                acc[...] += value

            @pl.when(h == per - 1)
            def _():
                lanes = lax.broadcasted_iota(jnp.int32, (128, 128), 1)
                both = jnp.where(lanes < ka, acc[:128, :], acc[128:, :])
                for p in range(dn):
                    part[e, p] = both[p * cm:(p + 1) * cm]
                for off in range(1, dn):
                    across(e, off).start()

        return carry

    lax.fori_loop(0, blocks + tail, step, 0)

    for e in range(examples):
        value = part[e, d]
        for off in range(1, dn):
            across(e, off).wait_recv()
            value = value + part_in[e, off - 1]
        ybuf[e * cm:(e + 1) * cm, :] = value
    turned = ybuf[...].T
    turned = turned[:ka] + turned[ka:]
    for p in range(zn):
        zbuf[p] = turned[p * rm:(p + 1) * rm]
    for off in range(1, zn):
        along(off).start()
    value = zbuf[z]
    for off in range(1, zn):
        along(off).wait_recv()
        value = value + zin[off - 1]
    value = value * scale
    for e in range(examples):
        out[e] = value[:, e * cm:(e + 1) * cm]

    for off in range(1, zn):
        along(off).wait_send()
    for e in range(examples):
        for off in range(1, dn):
            across(e, off).wait_send()

    def drain(k, carry):
        @pl.when(z < zn - 1)
        def _():
            up(k).wait_send()

        @pl.when(z > 0)
        def _():
            down(k).wait_send()

        return carry

    lax.fori_loop(0, chunks, drain, 0)


def local(acts, grads, lengths, row_sign, col_sign, row_index, col_index):
    examples, tokens, row_block = acts.shape
    col_block = grads.shape[2]
    zn = lax.axis_size("param")
    dn = lax.axis_size("dp")
    ka = row_index.shape[0]
    kb = col_index.shape[0]
    rm, cm = ka // zn, kb // dn
    scale = 1.0 / (D**0.5 * F**0.5 * (tokens * dn) ** 0.5)
    blocks = examples * tokens // BLK
    line = pltpu.VMEM((2 * blocks, SUB, 128), jnp.float32)
    dma = pltpu.SemaphoreType.DMA
    vmem = pl.BlockSpec(memory_space=pltpu.VMEM)
    hbm = pl.BlockSpec(memory_space=pl.ANY)
    return pl.pallas_call(
        functools.partial(kernel, zn, dn, scale),
        out_shape=jax.ShapeDtypeStruct((examples, rm, cm), jnp.float32),
        in_specs=[pl.BlockSpec(memory_space=pltpu.SMEM), vmem, vmem, vmem, vmem, hbm, hbm],
        out_specs=vmem,
        scratch_shapes=[
            pltpu.VMEM((row_block, 128), jnp.bfloat16),
            pltpu.VMEM((col_block, kb), jnp.bfloat16),
            pltpu.VMEM((SLOTS, BLK, row_block), jnp.bfloat16),
            pltpu.VMEM((SLOTS, BLK, col_block), jnp.bfloat16),
            line, line, line, line, line,
            pltpu.VMEM((blocks, 256, HALF), jnp.bfloat16),
            pltpu.VMEM((blocks, 256, HALF), jnp.bfloat16),
            pltpu.VMEM((256, 128), jnp.float32),
            pltpu.VMEM((examples, dn, cm, 128), jnp.float32),
            pltpu.VMEM((examples, dn - 1, cm, 128), jnp.float32),
            pltpu.VMEM((examples * cm, 128), jnp.float32),
            pltpu.VMEM((zn, rm, examples * cm), jnp.float32),
            pltpu.VMEM((zn - 1, rm, examples * cm), jnp.float32),
            dma((SLOTS,)), dma((SLOTS,)),
            dma((2 * blocks,)), dma((2 * blocks,)), dma((2 * blocks,)), dma((2 * blocks,)),
            dma((examples, dn - 1)), dma((examples, dn - 1)),
            dma((zn - 1,)), dma((zn - 1,)),
        ],
        compiler_params=pltpu.CompilerParams(
            collective_id=0, has_side_effects=True, vmem_limit_bytes=52 * 1024 * 1024
        ),
        cost_estimate=pl.CostEstimate(
            flops=2 * examples * tokens * (row_block * ka + col_block * kb),
            bytes_accessed=2 * examples * tokens * (row_block + col_block),
            transcendentals=0,
        ),
    )(
        lengths,
        row_sign.reshape(-1, 128),
        col_sign.reshape(-1, 128),
        jnp.concatenate([row_index] * (128 // ka)).reshape(1, 128),
        col_index.reshape(1, 128),
        acts,
        grads,
    )


def solution(mesh):
    placed = (
        P("groups", "dp", "param"),
        P("groups", "dp", "param"),
        P("groups"),
        P("param"),
        P("param"),
        P(),
        P(),
    )
    return jax.shard_map(
        local, mesh=mesh, in_specs=placed, out_specs=P("groups", "param", "dp"), check_vma=False
    )
```

```python
import functools

import jax
import jax.numpy as jnp
from jax import lax
from jax.experimental import pallas as pl
from jax.experimental.pallas import tpu as pltpu
from jax.sharding import PartitionSpec as P

D = 8192
F = 16384
BLK = 512
HALF = BLK // 2
SUB = HALF // 2
LAG = 3
SLOTS = 4
DELAY = 2


def hadamard_signs(base, stride, count, index):
    values = base + stride * lax.broadcasted_iota(jnp.int32, (count, 128), 0)
    values = jnp.bitwise_and(values, index)
    for shift in (16, 8, 4, 2, 1):
        values = jnp.bitwise_xor(values, jnp.right_shift(values, shift))
    return (1 - 2 * jnp.bitwise_and(values, 1)).astype(jnp.float32)


def split(x):
    hi = x.astype(jnp.bfloat16)
    return hi, (x - hi.astype(jnp.float32)).astype(jnp.bfloat16)


def dot(a, b):
    return jnp.dot(a, b, preferred_element_type=jnp.float32)


def kernel(zn, dn, scale, lengths, rsign, csign, rindex, cindex, acts, grads, out, rtab, ctab, abuf, gbuf, own, pin, sin,
           pout, sout, chi, clo, acc, part, part_in, ybuf, zbuf, zin, asem, gsem, psend, precv,
           ssend, srecv, dsend, drecv, zsend, zrecv):
    z = lax.axis_index("param")
    d = lax.axis_index("dp")
    examples, tokens, _ = acts.shape
    per = tokens // BLK
    blocks = examples * per
    chunks = 2 * blocks
    tail = (LAG * (zn - 1) + 1) // 2
    delay = min(tail, DELAY)
    cm = part.shape[2]
    rm = zbuf.shape[1]
    ka = 64

    def fetch(src, buf, sem, j):
        slot = lax.rem(j, SLOTS)
        rows = pl.ds(pl.multiple_of(lax.rem(j, per) * BLK, BLK), BLK)
        return pltpu.make_async_copy(src.at[j // per, rows, :], buf.at[slot], sem.at[slot])

    for j in range(min(SLOTS, blocks)):
        fetch(acts, abuf, asem, jnp.int32(j)).start()
        fetch(grads, gbuf, gsem, jnp.int32(j)).start()

    barrier = pltpu.get_barrier_semaphore()
    for off in range(1, zn):
        pl.semaphore_signal(barrier, inc=1, device_id={"param": lax.rem(z + off, zn)},
                            device_id_type=pl.DeviceIdType.MESH)
    for off in range(1, dn):
        pl.semaphore_signal(barrier, inc=1, device_id={"dp": lax.rem(d + off, dn)},
                            device_id_type=pl.DeviceIdType.MESH)
    def fill(sign, index, store):
        groups = sign.shape[0]
        high = hadamard_signs(z * groups * 128, 128, groups, index[...])
        low = hadamard_signs(0, 1, 128, index[...])
        flips = (1 - 2 * sign[...]).astype(jnp.float32).T
        for g in range(groups):
            store(g * 128, (low * high[g:g + 1, :]) * flips[:, g:g + 1])

    def store_rows(at, value):
        rtab[at:at + 128, :] = value.astype(jnp.bfloat16)

    def store_cols(at, value):
        ctab[at:at + 128, :] = value.astype(jnp.bfloat16)

    fill(rsign, rindex, store_rows)
    fill(csign, cindex, store_cols)
    pl.semaphore_wait(barrier, zn - 1 + dn - 1)

    def up(k):
        return pltpu.make_async_remote_copy(
            src_ref=pout.at[k], dst_ref=pin.at[k], send_sem=psend.at[k], recv_sem=precv.at[k],
            device_id={"param": lax.rem(z + 1, zn)}, device_id_type=pl.DeviceIdType.MESH)

    def down(k):
        return pltpu.make_async_remote_copy(
            src_ref=sout.at[k], dst_ref=sin.at[k], send_sem=ssend.at[k], recv_sem=srecv.at[k],
            device_id={"param": lax.rem(z + zn - 1, zn)}, device_id_type=pl.DeviceIdType.MESH)

    def across(e, off):
        peer = lax.rem(d + off, dn)
        return pltpu.make_async_remote_copy(
            src_ref=part.at[e, peer], dst_ref=part_in.at[e, off - 1],
            send_sem=dsend.at[e, off - 1], recv_sem=drecv.at[e, off - 1],
            device_id={"dp": peer}, device_id_type=pl.DeviceIdType.MESH)

    def along(off):
        peer = lax.rem(z + off, zn)
        return pltpu.make_async_remote_copy(
            src_ref=zbuf.at[peer], dst_ref=zin.at[off - 1],
            send_sem=zsend.at[off - 1], recv_sem=zrecv.at[off - 1],
            device_id={"param": peer}, device_id_type=pl.DeviceIdType.MESH)

    def one_way(t, place, copy, arrived, leaving):
        k = t - LAG * place

        @pl.when(jnp.logical_and(k >= 0, k < chunks))
        def _():
            @pl.when(place > 0)
            def _():
                copy(k).wait_recv()

            @pl.when(place == 0)
            def _():
                arrived[k] = jnp.zeros((SUB, 128), jnp.float32)

            @pl.when(place < zn - 1)
            def _():
                leaving[k] = own[k] + arrived[k]
                copy(k).start()

    def exchange(t):
        one_way(t, z, up, pin, pout)
        one_way(t, zn - 1 - z, down, sin, sout)

    lane = lax.broadcasted_iota(jnp.int32, (HALF, 128), 1)
    row = lax.broadcasted_iota(jnp.int32, (HALF, 128), 0)
    place = d * tokens + row + jnp.where(lane >= ka, HALF, 0)

    def step(j, carry):
        @pl.when(j < blocks)
        def _():
            slot = lax.rem(j, SLOTS)
            fetch(acts, abuf, asem, j).wait()
            value = jnp.where(
                lane < ka, dot(abuf[slot, :HALF, :], rtab[...]), dot(abuf[slot, HALF:, :], rtab[...])
            )
            live = place + lax.rem(j, per) * BLK < lengths[j // per]
            value = jnp.where(live, value, 0.0)
            own[2 * j] = value[:SUB]
            own[2 * j + 1] = value[SUB:]

            @pl.when(j + SLOTS < blocks)
            def _():
                fetch(acts, abuf, asem, j + SLOTS).start()

        exchange(2 * j)

        c = j - delay

        @pl.when(jnp.logical_and(c >= 0, c < blocks))
        def _():
            slot = lax.rem(c, SLOTS)
            fetch(grads, gbuf, gsem, c).wait()
            for half in range(2):
                value = dot(gbuf[slot, half * HALF:(half + 1) * HALF, :], ctab[...])
                hi, lo = split(value.T)
                chi[c, half * 128:(half + 1) * 128, :] = hi
                clo[c, half * 128:(half + 1) * 128, :] = lo

            @pl.when(c + SLOTS < blocks)
            def _():
                fetch(grads, gbuf, gsem, c + SLOTS).start()

        exchange(2 * j + 1)

        @pl.when(j >= tail)
        def _():
            b = j - tail
            e = b // per
            h = lax.rem(b, per)
            total = jnp.concatenate(
                [own[2 * b + s] + pin[2 * b + s] + sin[2 * b + s] for s in range(2)], axis=0)
            hi, lo = split(total)
            value = dot(chi[b], hi) + (dot(chi[b], lo) + dot(clo[b], hi))

            @pl.when(h == 0)
            def _():
                acc[...] = value

            @pl.when(h > 0)
            def _():
                acc[...] += value

            @pl.when(h == per - 1)
            def _():
                lanes = lax.broadcasted_iota(jnp.int32, (128, 128), 1)
                both = jnp.where(lanes < ka, acc[:128, :], acc[128:, :])
                for p in range(dn):
                    part[e, p] = both[p * cm:(p + 1) * cm]
                for off in range(1, dn):
                    across(e, off).start()

        return carry

    lax.fori_loop(0, blocks + tail, step, 0)

    for e in range(examples):
        value = part[e, d]
        for off in range(1, dn):
            across(e, off).wait_recv()
            value = value + part_in[e, off - 1]
        ybuf[e * cm:(e + 1) * cm, :] = value
    turned = ybuf[...].T
    turned = turned[:ka] + turned[ka:]
    for p in range(zn):
        zbuf[p] = turned[p * rm:(p + 1) * rm]
    for off in range(1, zn):
        along(off).start()
    value = zbuf[z]
    for off in range(1, zn):
        along(off).wait_recv()
        value = value + zin[off - 1]
    value = value * scale
    for e in range(examples):
        out[e] = value[:, e * cm:(e + 1) * cm]

    for off in range(1, zn):
        along(off).wait_send()
    for e in range(examples):
        for off in range(1, dn):
            across(e, off).wait_send()

    def drain(k, carry):
        @pl.when(z < zn - 1)
        def _():
            up(k).wait_send()

        @pl.when(z > 0)
        def _():
            down(k).wait_send()

        return carry

    lax.fori_loop(0, chunks, drain, 0)


def local(acts, grads, lengths, row_sign, col_sign, row_index, col_index):
    examples, tokens, row_block = acts.shape
    col_block = grads.shape[2]
    zn = lax.axis_size("param")
    dn = lax.axis_size("dp")
    ka = row_index.shape[0]
    kb = col_index.shape[0]
    rm, cm = ka // zn, kb // dn
    scale = 1.0 / (D**0.5 * F**0.5 * (tokens * dn) ** 0.5)
    blocks = examples * tokens // BLK
    line = pltpu.VMEM((2 * blocks, SUB, 128), jnp.float32)
    dma = pltpu.SemaphoreType.DMA
    vmem = pl.BlockSpec(memory_space=pltpu.VMEM)
    hbm = pl.BlockSpec(memory_space=pl.ANY)
    return pl.pallas_call(
        functools.partial(kernel, zn, dn, scale),
        out_shape=jax.ShapeDtypeStruct((examples, rm, cm), jnp.float32),
        in_specs=[pl.BlockSpec(memory_space=pltpu.SMEM), vmem, vmem, vmem, vmem, hbm, hbm],
        out_specs=vmem,
        scratch_shapes=[
            pltpu.VMEM((row_block, 128), jnp.bfloat16),
            pltpu.VMEM((col_block, kb), jnp.bfloat16),
            pltpu.VMEM((SLOTS, BLK, row_block), jnp.bfloat16),
            pltpu.VMEM((SLOTS, BLK, col_block), jnp.bfloat16),
            line, line, line, line, line,
            pltpu.VMEM((blocks, 256, HALF), jnp.bfloat16),
            pltpu.VMEM((blocks, 256, HALF), jnp.bfloat16),
            pltpu.VMEM((256, 128), jnp.float32),
            pltpu.VMEM((examples, dn, cm, 128), jnp.float32),
            pltpu.VMEM((examples, dn - 1, cm, 128), jnp.float32),
            pltpu.VMEM((examples * cm, 128), jnp.float32),
            pltpu.VMEM((zn, rm, examples * cm), jnp.float32),
            pltpu.VMEM((zn - 1, rm, examples * cm), jnp.float32),
            dma((SLOTS,)), dma((SLOTS,)),
            dma((2 * blocks,)), dma((2 * blocks,)), dma((2 * blocks,)), dma((2 * blocks,)),
            dma((examples, dn - 1)), dma((examples, dn - 1)),
            dma((zn - 1,)), dma((zn - 1,)),
        ],
        compiler_params=pltpu.CompilerParams(
            collective_id=0, has_side_effects=True, vmem_limit_bytes=52 * 1024 * 1024
        ),
        cost_estimate=pl.CostEstimate(
            flops=2 * examples * tokens * (row_block * ka + col_block * kb),
            bytes_accessed=2 * examples * tokens * (row_block + col_block),
            transcendentals=0,
        ),
    )(
        lengths,
        row_sign.reshape(-1, 128),
        col_sign.reshape(-1, 128),
        jnp.concatenate([row_index] * (128 // ka)).reshape(1, 128),
        col_index.reshape(1, 128),
        acts,
        grads,
    )


def solution(mesh):
    placed = (
        P("groups", "dp", "param"),
        P("groups", "dp", "param"),
        P("groups"),
        P("param"),
        P("param"),
        P(),
        P(),
    )
    return jax.shard_map(
        local, mesh=mesh, in_specs=placed, out_specs=P("groups", "param", "dp"), check_vma=False
    )
```
